32 devices in a mesh: row: 8 (over y, x, core), col: 4 (over z).
Axes of the slice: x: 2, y: 2, z: 4, core: 2. Of those that a mesh axis runs over, the one named last changes fastest.
Arguments:
- rhs: bfloat16 [5, 8, 32, 256], P(None, 'row'), may hold values from -6 to 6
- factor: bfloat16 [10, 8, 8, 256, 256], P(None, 'col', 'row'), may hold values from -0.125 to 0.125
- pattern: int32 [10, 8, 8], P(None, 'col', 'row'), may hold values 0 or 1
- diag_inverse: bfloat16 [5, 8, 256, 256], P(None, 'row'), as said below
Outputs:
- forward: bfloat16 [5, 8, 32, 256], P(None, 'row')
- solution: bfloat16 [5, 8, 32, 256], P(None, 'row')
The draws below stay inside these ranges and needn't reach their ends.
Inputs may be any that keep to these rules, and one draw needn't show every extreme that they name: Each block of diag_inverse is lower triangular with a positive diagonal.
All inputs are finite; a program needn't handle non-finite values. No bound on the sum of `pattern` on one device may be relied on, other than what follows from the above.
Results may differ from the reference program's by a relative error of at most 0.028.
Values may be sent and summed in bfloat16 or wider, within the bound.
No kernel may reach another device: no remote copies, remote signals or barrier semaphores. Data moves between devices by JAX's collectives and lax.ppermute only.
A program may use at most 64 MiB of HBM per device.

```python
import jax
import jax.numpy as jnp

W = 256
R = 32
LV = 5
M = 8
PAIRS = 10


def draw_diag_inverse(key, part):
    key_diag, key_low = jax.random.split(jax.random.fold_in(key, 17))
    diag = jnp.exp(jax.random.uniform(key_diag, (LV, M, W), jnp.float32, jnp.log(0.5), jnp.log(1.5)))
    low = jnp.clip(jax.random.normal(key_low, (LV, M, W, W), jnp.float32), -3.0, 3.0)
    rows = jnp.arange(W)[:, None]
    cols = jnp.arange(W)[None, :]
    strict = (rows > cols).astype(jnp.float32)
    unit = (rows == cols).astype(jnp.float32)
    values = low * (0.5 / jnp.sqrt(jnp.float32(W))) * strict + diag[:, :, :, None] * unit
    return values.astype(jnp.bfloat16)


def touch_ends(drawn, key, low, largest):
    index_at = [jax.random.randint(jax.random.fold_in(key, axis), (), 0, length) for axis, length in enumerate(drawn.shape)]
    main_axis = drawn.shape.index(max(drawn.shape))
    beside = index_at[:main_axis] + [(index_at[main_axis] + 1) % drawn.shape[main_axis]] + index_at[main_axis + 1:]
    return drawn.at[tuple(index_at)].set(low).at[tuple(beside)].set(largest)


def steps_of(stream_key, shape, cuts, smallest, largest):
    factor_of = 1.0
    for dim, shards_of in cuts:
        heights = jax.random.uniform(jax.random.fold_in(jax.random.fold_in(stream_key, 6), dim), (shards_of,), jnp.float32, smallest / len(cuts), largest / len(cuts))
        factor_of = factor_of * jnp.repeat(jnp.exp(heights), shape[dim] // shards_of).reshape((-1,) + (1,) * (len(shape) - 1 - dim))
    return factor_of


def normal_values(stream_key, dims, width, reach, cuts=(), held_as=jnp.bfloat16):
    gain = steps_of(stream_key, dims, cuts, -0.22, 0.18) if cuts else 1.0
    drawn = jax.random.normal(stream_key, dims, jnp.float32) * width * gain
    return jnp.minimum(jnp.maximum(drawn, -reach), reach).astype(held_as)


def setup_inputs(seed: int = 0) -> dict:
    keys = jax.random.split(jax.random.key(seed), 5)
    return {
        "rhs": normal_values(keys[0], (LV, M, R, W), 1.0, 6.0, ((1, 8),)),
        "factor": normal_values(keys[1], (PAIRS, M, M, W, W), (M * W * (LV - 1) // 4) ** -0.5, 0.125, ((1, 4), (2, 8))),
        "pattern": touch_ends((jax.random.randint(keys[2], (PAIRS, M, M), 0, 4) < 3).astype(jnp.int32), jax.random.fold_in(keys[2], 1), 0, 1),
        "diag_inverse": draw_diag_inverse(jax.random.fold_in(keys[4], 71), 0),
    }


def pair_index(later, earlier):
    return later * (later - 1) // 2 + earlier


def reference(rhs, factor, pattern, diag_inverse):
    mask_f = pattern.astype(jnp.float32)
    forward_list = []
    for level in range(LV):
        if level == 0:
            zeta = rhs[0]
        else:
            total = jnp.zeros((M, R, W), jnp.float32)
            for earlier in range(level):
                index = pair_index(level, earlier)
                blocks = factor[index].astype(jnp.float32)
                prod = jnp.einsum('tsij,srj->tsri', blocks, forward_list[earlier].astype(jnp.float32))
                total = total + jnp.sum(prod * mask_f[index][:, :, None, None], axis=1)
            zeta = (rhs[level].astype(jnp.float32) - total).astype(jnp.bfloat16)
        solved = jnp.einsum('mrj,mij->mri', zeta.astype(jnp.float32), diag_inverse[level].astype(jnp.float32))
        forward_list.append(solved.astype(jnp.bfloat16))
    back_list = [None] * LV
    for level in range(LV - 1, -1, -1):
        if level == LV - 1:
            zeta = forward_list[level]
        else:
            total = jnp.zeros((M, R, W), jnp.float32)
            for later in range(LV - 1, level, -1):
                index = pair_index(later, level)
                blocks = factor[index].astype(jnp.float32)
                prod = jnp.einsum('tri,tsij->tsrj', back_list[later].astype(jnp.float32), blocks)
                total = total + jnp.sum(prod * mask_f[index][:, :, None, None], axis=0)
            zeta = (forward_list[level].astype(jnp.float32) - total).astype(jnp.bfloat16)
        solved = jnp.einsum('mri,mij->mrj', zeta.astype(jnp.float32), diag_inverse[level].astype(jnp.float32))
        back_list[level] = solved.astype(jnp.bfloat16)
    return jnp.stack(forward_list), jnp.stack(back_list)
```

```python
import functools

import jax
import jax.numpy as jnp
from jax import lax
from jax.experimental import pallas as pl
from jax.experimental.pallas import tpu as pltpu
from jax.sharding import PartitionSpec as P

BOTH = ("row", "col")
NT = (((1,), (1,)), ((), ()))
NN = (((1,), (0,)), ((), ()))


def pair_index(later, earlier):
    return later * (later - 1) // 2 + earlier


def parity(q):
    return bin(q).count("1") & 1


def turn(q, z):
    return parity(q) ^ (z & 1)


def perm(n, target):
    pairs = []
    for q in range(n):
        for k in range(2):
            for z in range(n):
                to = target(q, k, z)
                if to == (q, k, z):
                    to = (q, k ^ 1, z)
                pairs.append(((2 * q + k) * n + z, (2 * to[0] + to[1]) * n + to[2]))
    return pairs


def plane_perms(n):
    return [perm(n, lambda q, k, z, m=m: (q ^ m, k ^ parity(m), z)) for m in range(1, n)]


def line_perms(n):
    return [perm(n, lambda q, k, z, m=m: (q, k ^ (m & 1), z ^ m)) for m in range(1, n)]


def chip_perm(n, chip):
    def target(q, k, z):
        a, b = chip(q, z)
        return a, k ^ turn(q, z) ^ turn(a, b), b

    return perm(n, target)


def down_perms(n):
    return [chip_perm(n, lambda q, z, j=j: (z, (q + j) % n)) for j in range(n)]


def up_perms(n):
    return [chip_perm(n, lambda q, z, j=j: ((z + j) % n, q)) for j in range(n)]


def turn_perm(n):
    return chip_perm(n, lambda q, z: (z, q))


def core_perm(n):
    return perm(n, lambda q, k, z: (q, k ^ 1, z))


def tree(parts):
    while len(parts) > 1:
        half = len(parts) // 2
        parts = [parts[i] + parts[i + half] for i in range(half)]
    return parts[0]


def f32(x):
    return x.astype(jnp.float32)


def bf16(x):
    return x.astype(jnp.bfloat16)


def dot(a, b, dims):
    return lax.dot_general(a, b, dims, preferred_element_type=jnp.float32)


def total_direct(info, own, got):
    first = jnp.where(info[1] == 1, f32(own[...]), f32(got[0][...]))
    return tree([first] + [f32(g[...]) for g in got[1:]])


def total_swap(own, got):
    return tree([f32(own[...])] + [f32(g[...]) for g in got])


def lower_part(info, pairs, solved, mine, other, mask, mask_other):
    k = info[0]
    outs = []
    for t in range(2):
        acc = None
        for p, y in zip(pairs, solved, strict=True):
            a = dot(y[k], mine[p, t], NT) * f32(mask[p, t])
            b = dot(y[1 - k], other[p, t], NT) * f32(mask_other[p, t])
            acc = a + b if acc is None else acc + (a + b)
        outs.append(acc)
    return outs


def upper_part(info, pairs, solved, mine, other, mask, mask_other):
    outs = []
    for blocks, m in ((mine, mask), (other, mask_other)):
        acc = None
        for p, x in zip(pairs, solved, strict=True):
            for t in range(2):
                a = dot(x[t], blocks[p, t], NN) * f32(m[p, t])
                acc = a if acc is None else acc + a
        outs.append(acc)
    return outs


def start_kernel(pairs, info, mask, mask_other, rhs, rhs_other, inv, inv_other, mine, other, y_ref, msg_ref):
    k = info[0]
    rows = pl.ds(pl.multiple_of(info[2] * 16, 16), 16)
    y_ref[k] = bf16(dot(rhs[0, rows, :], inv[0], NT))
    y_ref[1 - k] = bf16(dot(rhs_other[0, rows, :], inv_other[0], NT))
    for t, part in enumerate(lower_part(info, pairs, [y_ref], mine, other, mask, mask_other)):
        msg_ref[t] = bf16(part)


def down_kernel(level, n, pairs, *refs):
    info, mask, mask_other, rhs, rhs_other, inv, inv_other, mine, other, own = refs[:10]
    got, earlier = refs[10 : 10 + n], refs[10 + n : 10 + n + level]
    y_ref, msg_ref, total_ref = refs[10 + n + level :]
    k = info[0]
    rows = pl.ds(pl.multiple_of(info[2] * 16, 16), 16)
    total_ref[...] = total_direct(info, own, got)
    y_ref[k] = bf16(dot(bf16(f32(rhs[level, rows, :]) - total_ref[k]), inv[level], NT))
    y_ref[1 - k] = bf16(dot(bf16(f32(rhs_other[level, rows, :]) - total_ref[1 - k]), inv_other[level], NT))
    parts = lower_part(info, pairs, list(earlier) + [y_ref], mine, other, mask, mask_other)
    if level == 3:
        total_ref[k] = f32(rhs[level + 1, rows, :])
        total_ref[1 - k] = f32(rhs_other[level + 1, rows, :])
        parts = [jnp.where(info[1] == 1, p - total_ref[t], p) for t, p in enumerate(parts)]
    for t, part in enumerate(parts):
        msg_ref[t] = bf16(part)


def turn_kernel(n, pairs, *refs):
    info, mask, mask_other, inv, inv_other, mine, other, y3, own = refs[:9]
    got = refs[9 : 9 + n - 1]
    y_ref, x_ref, msg_ref = refs[9 + n - 1 :]
    k = info[0]
    zeta = bf16(-total_swap(own, got))
    x_ref[...] = zeta
    zk, zo = x_ref[k], x_ref[1 - k]
    y_ref[k] = bf16(dot(zk, inv[3], NT))
    y_ref[1 - k] = bf16(dot(zo, inv_other[3], NT))
    x_ref[k] = bf16(dot(y_ref[k], inv[3], NN))
    x_ref[1 - k] = bf16(dot(y_ref[1 - k], inv_other[3], NN))
    parts = upper_part(info, pairs, [x_ref], mine, other, mask, mask_other)
    for i, part in enumerate(parts):
        at = k if i == 0 else 1 - k
        msg_ref[at] = bf16(jnp.where(info[1] == 1, part - f32(y3[at]), part))


def up_kernel(level, n, pairs, *refs):
    info, mask, mask_other, inv, inv_other, mine, other, below, own = refs[:9]
    got, later = refs[9 : 9 + n], refs[9 + n : 9 + n + 4 - level]
    x_ref, msg_ref = refs[9 + n + 4 - level :]
    k = info[0]
    x_ref[...] = bf16(-total_direct(info, own, got))
    zk, zo = x_ref[k], x_ref[1 - k]
    x_ref[k] = bf16(dot(zk, inv[level - 1], NN))
    x_ref[1 - k] = bf16(dot(zo, inv_other[level - 1], NN))
    parts = upper_part(info, pairs, list(later) + [x_ref], mine, other, mask, mask_other)
    for i, part in enumerate(parts):
        at = k if i == 0 else 1 - k
        if level > 1:
            part = jnp.where(info[1] == 1, part - f32(below[at]), part)
        msg_ref[at] = bf16(part)


def last_kernel(n, *refs):
    info, inv, inv_other, y0, own = refs[:5]
    got = refs[5 : 5 + n - 1]
    x_ref, total_ref = refs[5 + n - 1 :]
    k = info[0]
    total_ref[...] = f32(y0[...]) - total_swap(own, got)
    x_ref[k] = bf16(dot(bf16(total_ref[k]), inv[0], NN))
    x_ref[1 - k] = bf16(dot(bf16(total_ref[1 - k]), inv_other[0], NN))


def call(body, outs, smem, vmem, scratch=()):
    return pl.pallas_call(
        body,
        out_shape=[jax.ShapeDtypeStruct(s, jnp.bfloat16) for s in outs],
        in_specs=[pl.BlockSpec(memory_space=pltpu.SMEM)] * len(smem)
        + [pl.BlockSpec(memory_space=pltpu.VMEM)] * len(vmem),
        out_specs=[pl.BlockSpec(memory_space=pltpu.VMEM)] * len(outs),
        scratch_shapes=[pltpu.VMEM(s, jnp.float32) for s in scratch],
        compiler_params=pltpu.CompilerParams(vmem_limit_bytes=40 * 1024 * 1024),
    )(*smem, *vmem)


def on_device(rhs, factor, pattern, diag_inverse):
    n = lax.axis_size("col")
    levels, own, count, width = rhs.shape
    assert levels == 5 and own == 1 and factor.shape[1] == 2 and lax.axis_size("row") == 2 * n
    row, z = lax.axis_index("row"), lax.axis_index("col")
    q, k = row // 2, row % 2
    bits = max(1, (n - 1).bit_length())
    odd = functools.reduce(jnp.bitwise_xor, [(q >> i) & 1 for i in range(bits)])
    half = k ^ odd ^ (z & 1)
    info = jnp.stack([k, (q == z).astype(jnp.int32), half]).astype(jnp.int32)

    rhs, inv = rhs[:, 0], diag_inverse[:, 0]
    mine, mask = factor[:, :, 0], pattern[:, :, 0]
    swap = functools.partial(lax.ppermute, axis_name=BOTH, perm=core_perm(n))
    send = lambda x, perms: [lax.ppermute(x, BOTH, p) for p in perms]
    rhs_o, mask_o, inv_o, other = swap(rhs), swap(mask), swap(inv), swap(mine)

    far = perm(n, lambda a, c, b: (b, c ^ 1, a))
    inv_to = lax.ppermute(inv[1:], BOTH, far)
    inv_tk = swap(inv_to)

    vec = (2, count // 2, width)
    masks = (info, mask, mask_o)
    y = [None] * 5
    x = [None] * 5
    y[0], msg = call(
        functools.partial(start_kernel, [pair_index(1, 0)]), [vec, vec], masks, (rhs, rhs_o, inv, inv_o, mine, other)
    )
    for level in range(1, 4):
        got = send(msg, down_perms(n))
        pairs = [pair_index(level + 1, b) for b in range(level + 1)]
        y[level], msg = call(
            functools.partial(down_kernel, level, n, pairs),
            [vec, vec],
            masks,
            (rhs, rhs_o, inv, inv_o, mine, other, msg, *got, *y[:level]),
            [vec],
        )
    got = send(msg, plane_perms(n))
    y[4], x[4], msg = call(
        functools.partial(turn_kernel, n, [pair_index(4, 3)]),
        [vec, vec, vec],
        masks,
        (inv_tk, inv_to, mine, other, y[3], msg, *got),
    )
    for level in (3, 2, 1):
        got = send(msg, up_perms(n))
        pairs = [pair_index(c, level - 1) for c in range(4, level - 1, -1)]
        x[level], msg = call(
            functools.partial(up_kernel, level, n, pairs),
            [vec, vec],
            masks,
            (inv_tk, inv_to, mine, other, y[level - 1], msg, *got, *x[4:level:-1]),
        )
    got = send(msg, line_perms(n))
    (x[0],) = call(functools.partial(last_kernel, n), [vec], (info,), (inv, inv_o, y[0], msg, *got), [vec])

    held = jnp.stack([y[4], x[4], x[3], x[2], x[1]])
    moved = lax.ppermute(held, BOTH, turn_perm(n))
    moved = jnp.where(q == z, held, moved)
    full = jnp.stack([*y[:4], moved[0], x[0], moved[4], moved[3], moved[2], moved[1]])
    keep = jnp.where(k == 0, full[:, 0], full[:, 1])
    give = jnp.where(k == 0, full[:, 1], full[:, 0])
    take = swap(give)
    low = jnp.where(half == 0, keep, take)
    high = jnp.where(half == 0, take, keep)
    out = jnp.concatenate([low, high], axis=1)[:, None]
    return out[:5], out[5:]


def solution(mesh):
    return jax.shard_map(
        on_device,
        mesh=mesh,
        in_specs=(
            P(None, "row", None, None),
            P(None, "col", "row", None, None),
            P(None, "col", "row"),
            P(None, "row", None, None),
        ),
        out_specs=(P(None, "row", None, None), P(None, "row", None, None)),
        check_vma=False,
    )
```

```python
import functools

import jax
import jax.numpy as jnp
from jax import lax
from jax.experimental import pallas as pl
from jax.experimental.pallas import tpu as pltpu
from jax.sharding import PartitionSpec as P

BOTH = ("row", "col")
NT = (((1,), (1,)), ((), ()))
NN = (((1,), (0,)), ((), ()))


def pair_index(later, earlier):
    return later * (later - 1) // 2 + earlier


def perm(n, target):
    pairs = []
    for q in range(n):
        for k in range(2):
            for z in range(n):
                a, b, c = target(q, k, z)
                assert (a, b, c) != (q, k, z)
                pairs.append(((2 * q + k) * n + z, (2 * a + b) * n + c))
    return pairs


def down_perms(n):
    return [perm(n, lambda q, k, z, j=j: (z, (q & 1) ^ 1, 2 * ((q >> 1) ^ j) + k)) for j in range(n // 2)]


def up_perms(n):
    return [perm(n, lambda q, k, z, j=j: (2 * ((z >> 1) ^ j) + k, (z & 1) ^ 1, q)) for j in range(n // 2)]


def plane_perms(n):
    return [perm(n, lambda q, k, z, m=m: (q ^ m, k ^ (m.bit_count() & 1), z)) for m in range(1, n)]


def line_perms(n):
    return [perm(n, lambda q, k, z, m=m: (q, k ^ (m & 1), z ^ m)) for m in range(1, n)]


def turn_perm(n):
    return perm(n, lambda q, k, z: (z, k ^ 1, q ^ z))


def far_perm(n):
    return perm(n, lambda q, k, z: (q ^ z, k ^ 1, q))


def core_perm(n):
    return perm(n, lambda q, k, z: (q, k ^ 1, z))


def tree(parts):
    while len(parts) > 1:
        half = len(parts) // 2
        parts = [parts[i] + parts[i + half] for i in range(half)]
    return parts[0]


def f32(x):
    return x.astype(jnp.float32)


def bf16(x):
    return x.astype(jnp.bfloat16)


def dot(a, b, dims):
    return lax.dot_general(a, b, dims, preferred_element_type=jnp.float32)


def place():
    row = lax.axis_index("row")
    return row % 2, row // 2 == lax.axis_index("col")


def row_of(mask, p, t):
    return mask[3, pl.ds(2 * p + t, 1), :]


def lower_part(k, pairs, solved, mine, other, keep, gotten):
    outs = []
    for t in range(2):
        acc = None
        for p, y in zip(pairs, solved, strict=True):
            a = dot(y[k], mine[p, t], NT) * row_of(keep, p, t)
            b = dot(y[1 - k], other[p, t], NT) * row_of(gotten, p, t)
            acc = a + b if acc is None else acc + (a + b)
        outs.append(acc)
    return outs


def upper_part(pairs, solved, mine, other, keep, gotten):
    outs = []
    for blocks, mask in ((mine, keep), (other, gotten)):
        acc = None
        for p, x in zip(pairs, solved, strict=True):
            for t in range(2):
                a = dot(x[t], blocks[p, t], NN) * row_of(mask, p, t)
                acc = a if acc is None else acc + a
        outs.append(acc)
    return outs


def start_kernel(pattern, rhs, inv, mine, keep_ref, give_ref, rhs_in, inv_in, mine_in, sems):
    copies = [
        pltpu.make_async_copy(source.at[0], target, sems.at[i])
        for i, (source, target) in enumerate(((rhs, rhs_in), (inv, inv_in), (mine, mine_in)))
    ]
    for copy in copies:
        copy.start()
    for i in range(keep_ref.shape[1]):
        value = f32(pattern[i % 2, 0, i // 2]) if i < 2 * pattern.shape[2] else 0.0
        keep_ref[3, pl.ds(i, 1), :] = jnp.full((1, keep_ref.shape[2]), value, jnp.float32)
    for copy in copies:
        copy.wait()
    y = bf16(dot(rhs_in[...], inv_in[...], NT))
    keep_ref[0] = f32(y)
    for t in range(2):
        keep_ref[1 + t] = dot(y, mine_in[t], NT) * f32(pattern[t, 0, 0])
    give_ref[...] = keep_ref[...]


def join_kernel(keep, gotten, inv, mine, y_ref, msg_ref):
    del inv, mine
    k, _ = place()
    y_ref[k] = bf16(keep[0])
    y_ref[1 - k] = bf16(gotten[0])
    for t in range(2):
        msg_ref[t] = bf16(keep[1 + t] + gotten[1 + t])


def stage_kernel(*refs):
    count = (len(refs) - 1) // 2
    sems, copies = refs[-1], []
    for source, target in zip(refs[:count], refs[count:-1], strict=True):
        for i in range(source.shape[0]):
            copies.append(pltpu.make_async_copy(source.at[i], target.at[i], sems.at[len(copies)]))
    for copy in copies:
        copy.start()
    for copy in copies:
        copy.wait()


def down_kernel(level, pairs, *refs):
    keep, gotten, rhs, rhs_other, inv, inv_other, mine, other, some, rest = refs[:10]
    earlier = refs[10 : 10 + level]
    y_ref, msg_ref, total_ref = refs[10 + level :]
    k, diagonal = place()
    total_ref[...] = some[...] + rest[...]
    for at, b, inverse in ((k, rhs, inv), (1 - k, rhs_other, inv_other)):
        y_ref[at] = bf16(dot(bf16(f32(b[level]) - total_ref[at]), inverse[level], NT))
    parts = lower_part(k, pairs, list(earlier) + [y_ref], mine, other, keep, gotten)
    if level == 3:
        total_ref[k], total_ref[1 - k] = f32(rhs[4]), f32(rhs_other[4])
        parts = [jnp.where(diagonal, p - total_ref[t], p) for t, p in enumerate(parts)]
    for t, part in enumerate(parts):
        msg_ref[t] = bf16(part)


def up_parts(k, diagonal, level, pairs, solved, y, factors, inv, inv_other):
    parts = upper_part(pairs, solved, *factors)
    outs = []
    for part, at, inverse in zip(parts, (k, 1 - k), (inv, inv_other), strict=True):
        part = jnp.where(diagonal, part - f32(y[at]), part)
        outs.append((at, bf16(dot(bf16(part), inverse[level], NN))))
    return outs


def turn_kernel(n, pairs, *refs):
    keep, gotten, inv_k, inv_o, inv, inv_other, mine, other, y3, own = refs[:10]
    got = refs[10 : 10 + n - 1]
    y_ref, x_ref, msg_ref = refs[10 + n - 1 :]
    k, diagonal = place()
    x_ref[...] = bf16(-tree([f32(own[...])] + [f32(g[...]) for g in got]))
    for at, inverse in ((k, inv_k), (1 - k, inv_o)):
        y_ref[at] = bf16(dot(x_ref[at], inverse[...], NT))
    for at, inverse in ((k, inv_k), (1 - k, inv_o)):
        x_ref[at] = bf16(dot(y_ref[at], inverse[...], NN))
    for at, part in up_parts(k, diagonal, 3, pairs, [x_ref], y3, (mine, other, keep, gotten), inv, inv_other):
        msg_ref[at] = part


def up_kernel(level, pairs, *refs):
    keep, gotten, inv, inv_other, mine, other, below, y4, some, rest = refs[:10]
    later = refs[10 : 14 - level]
    outs = refs[14 - level :]
    k, diagonal = place()
    x_ref = outs[0]
    x_ref[...] = bf16(-(some[...] + rest[...]))
    solved = list(later) + [x_ref]
    parts = up_parts(k, diagonal, level - 1, pairs, solved, below, (mine, other, keep, gotten), inv, inv_other)
    if level > 1:
        for at, part in parts:
            outs[1][at] = part
    else:
        for ref, (_, part) in zip(outs[1:], parts, strict=False):
            ref[...] = part
        for i, v in enumerate((y4, *solved)):
            outs[3][i] = v[1 - k]


def out_kernel(n, *refs):
    own, got = refs[0], refs[1:n]
    y, moved = refs[n : n + 4], refs[n + 4]
    forward, solved, forward_ref, solved_ref, sems = refs[n + 5 :]
    k, _ = place()
    for level in range(4):
        forward_ref[level, 0] = y[level][k]
        solved_ref[4 - level, 0] = moved[1 + level]
    forward_ref[4, 0] = moved[0]
    solved_ref[0, 0] = bf16(-tree([f32(own[...])] + [f32(g[...]) for g in got]))
    copies = [
        pltpu.make_async_copy(forward_ref, forward, sems.at[0]),
        pltpu.make_async_copy(solved_ref, solved, sems.at[1]),
    ]
    for copy in copies:
        copy.start()
    for copy in copies:
        copy.wait()


VMEM = pl.BlockSpec(memory_space=pltpu.VMEM)
ANY = pl.BlockSpec(memory_space=pl.ANY)
ROOM = pltpu.CompilerParams(vmem_limit_bytes=16 * 1024 * 1024)


def call(body, outs, args, scratch=()):
    return pl.pallas_call(
        body,
        out_shape=[jax.ShapeDtypeStruct(s, jnp.bfloat16) for s in outs],
        in_specs=[VMEM] * len(args),
        out_specs=[VMEM] * len(outs),
        scratch_shapes=list(scratch),
        compiler_params=ROOM,
    )(*args)


def on_device(rhs, factor, pattern, diag_inverse):
    n = lax.axis_size("col")
    levels, own, count, width = rhs.shape
    assert levels == 5 and own == 1 and factor.shape[1] == 2 and lax.axis_size("row") == 2 * n

    rhs, inv = rhs[:, 0], diag_inverse[:, 0]
    mine = factor[:, :, 0]
    swap = functools.partial(lax.ppermute, axis_name=BOTH, perm=core_perm(n))
    send = lambda x, perms: [lax.ppermute(x, BOTH, p) for p in perms]
    vec, slots = (2, count, width), (4, count, width)

    def share(msg, perms):
        got = send(msg, perms)
        some = tree([f32(g) for g in got])
        return got, some, swap(some)

    last, rhs_first = lax.optimization_barrier((inv[4], rhs))
    inv_to = lax.ppermute(last, BOTH, far_perm(n))
    inv_o, other, rhs_o = swap(inv), swap(mine), swap(rhs)
    keep, give = pl.pallas_call(
        start_kernel,
        out_shape=[jax.ShapeDtypeStruct(slots, jnp.float32)] * 2,
        in_specs=[pl.BlockSpec(memory_space=pltpu.SMEM), ANY, ANY, ANY],
        out_specs=[VMEM] * 2,
        scratch_shapes=[pltpu.VMEM(a.shape[1:], a.dtype) for a in (rhs, inv, mine)] + [pltpu.SemaphoreType.DMA((3,))],
        compiler_params=ROOM,
    )(pattern.transpose(1, 2, 0), rhs_first, inv, mine)
    gotten = swap(give)

    y = [None] * 5
    x = [None] * 5
    y[0], msg = call(join_kernel, [vec, vec], (keep, gotten, inv, mine))
    for level in range(1, 4):
        got, some, rest = share(msg, down_perms(n))
        if level == 1:
            inv_o, other, _ = lax.optimization_barrier((inv_o, other, got[0]))
            inv_o, other = pl.pallas_call(
                stage_kernel,
                out_shape=[jax.ShapeDtypeStruct(a.shape, a.dtype) for a in (inv_o, other)],
                in_specs=[ANY] * 2,
                out_specs=[VMEM] * 2,
                scratch_shapes=[pltpu.SemaphoreType.DMA((inv_o.shape[0] + other.shape[0],))],
                compiler_params=ROOM,
            )(inv_o, other)
            inv_tk = swap(inv_to)
        pairs = [pair_index(level + 1, b) for b in range(level + 1)]
        y[level], msg = call(
            functools.partial(down_kernel, level, pairs),
            [vec, vec],
            (keep, gotten, rhs, rhs_o, inv, inv_o, mine, other, some, rest, *y[:level]),
            [pltpu.VMEM(vec, jnp.float32)],
        )
    got = send(msg, plane_perms(n))
    y[4], x[4], msg = call(
        functools.partial(turn_kernel, n, [pair_index(4, 3)]),
        [vec, vec, vec],
        (keep, gotten, inv_tk, inv_to, inv, inv_o, mine, other, y[3], msg, *got),
    )
    for level in (3, 2, 1):
        got, some, rest = share(msg, up_perms(n))
        pairs = [pair_index(c, level - 1) for c in range(4, level - 1, -1)]
        x[level], msg, *more = call(
            functools.partial(up_kernel, level, pairs),
            [vec, vec] if level > 1 else [vec, vec[1:], vec[1:], (5, *vec[1:])],
            (keep, gotten, inv, inv_o, mine, other, y[level - 1], y[4], some, rest, *x[4:level:-1]),
        )
    moved = lax.ppermute(more[1], BOTH, turn_perm(n))
    got = [lax.ppermute(more[0] if m & 1 else msg, BOTH, p) for m, p in enumerate(line_perms(n), 1)]
    out = jax.ShapeDtypeStruct((levels, 1, count, width), jnp.bfloat16)
    return pl.pallas_call(
        functools.partial(out_kernel, n),
        out_shape=[out, out],
        in_specs=[VMEM] * (n + 5),
        out_specs=[ANY] * 2,
        scratch_shapes=[pltpu.VMEM(out.shape, out.dtype)] * 2 + [pltpu.SemaphoreType.DMA((2,))],
        compiler_params=ROOM,
    )(msg, *got, *y[:4], moved)


def solution(mesh):
    return jax.shard_map(
        on_device,
        mesh=mesh,
        in_specs=(
            P(None, "row", None, None),
            P(None, "col", "row", None, None),
            P(None, "col", "row"),
            P(None, "row", None, None),
        ),
        out_specs=(P(None, "row", None, None), P(None, "row", None, None)),
        check_vma=False,
    )
```

```python
import functools

import jax
import jax.numpy as jnp
from jax import lax
from jax.experimental import pallas as pl
from jax.experimental.pallas import tpu as pltpu
from jax.sharding import PartitionSpec as P

BOTH = ("row", "col")
NT = (((1,), (1,)), ((), ()))
NN = (((1,), (0,)), ((), ()))


def pair_index(later, earlier):
    return later * (later - 1) // 2 + earlier


def perm(n, target):
    pairs = []
    for q in range(n):
        for k in range(2):
            for z in range(n):
                a, b, c = target(q, k, z)
                assert (a, b, c) != (q, k, z)
                pairs.append(((2 * q + k) * n + z, (2 * a + b) * n + c))
    return pairs


def down_perms(n):
    return [perm(n, lambda q, k, z, j=j: (z, (q & 1) ^ 1, 2 * ((q >> 1) ^ j) + k)) for j in range(n // 2)]


def up_perms(n):
    return [perm(n, lambda q, k, z, j=j: (2 * ((z >> 1) ^ j) + k, (z & 1) ^ 1, q)) for j in range(n // 2)]


def plane_perms(n):
    return [perm(n, lambda q, k, z, m=m: (q ^ m, k ^ (m.bit_count() & 1), z)) for m in range(1, n)]


def line_perms(n):
    return [perm(n, lambda q, k, z, m=m: (q, k ^ (m & 1), z ^ m)) for m in range(1, n)]


def turn_perm(n):
    return perm(n, lambda q, k, z: (z, k ^ 1, q ^ (n - 1)))


def far_perm(n):
    return perm(n, lambda q, k, z: (z ^ (n - 1), k ^ 1, q))


def core_perm(n):
    return perm(n, lambda q, k, z: (q, k ^ 1, z))


def tree(parts):
    while len(parts) > 1:
        half = len(parts) // 2
        parts = [parts[i] + parts[i + half] for i in range(half)]
    return parts[0]


def f32(x):
    return x.astype(jnp.float32)


def bf16(x):
    return x.astype(jnp.bfloat16)


def dot(a, b, dims):
    return lax.dot_general(a, b, dims, preferred_element_type=jnp.float32)


def place():
    row = lax.axis_index("row")
    return row % 2, row // 2 == lax.axis_index("col")


def row_of(mask, p, t):
    return mask[3, pl.ds(2 * p + t, 1), :]


def lower_part(k, pairs, solved, mine, other, keep, gotten):
    outs = []
    for t in range(2):
        acc = None
        for p, y in zip(pairs, solved, strict=True):
            a = dot(y[k], mine[p, t], NT) * row_of(keep, p, t)
            b = dot(y[1 - k], other[p, t], NT) * row_of(gotten, p, t)
            acc = a + b if acc is None else acc + (a + b)
        outs.append(acc)
    return outs


def upper_part(pairs, solved, mine, other, keep, gotten):
    outs = []
    for blocks, mask in ((mine, keep), (other, gotten)):
        acc = None
        for p, x in zip(pairs, solved, strict=True):
            for t in range(2):
                a = dot(x[t], blocks[p, t], NN) * row_of(mask, p, t)
                acc = a if acc is None else acc + a
        outs.append(acc)
    return outs


def start_kernel(pattern, rhs, inv, last, mine, keep_ref, give_ref, last_ref):
    low = last.shape[1] // 2
    last_ref[:low] = last[0, low:, :]
    last_ref[low:, :low] = last[0, : low // 2, :low]
    last_ref[low:, low:] = last[0, low // 2 : low, :low]
    y = bf16(dot(rhs[0], inv[0], NT))
    keep_ref[0] = f32(y)
    for t in range(2):
        keep_ref[1 + t] = dot(y, mine[0, t], NT) * f32(pattern[t, 0, 0])
    for i in range(keep_ref.shape[1]):
        value = f32(pattern[i % 2, 0, i // 2]) if i < 2 * pattern.shape[2] else 0.0
        keep_ref[3, pl.ds(i, 1), :] = jnp.full((1, keep_ref.shape[2]), value, jnp.float32)
    give_ref[...] = keep_ref[...]


def start_all(sems, moves):
    copies = [pltpu.make_async_copy(a, b, sems.at[i]) for i, (a, b) in enumerate(moves)]
    for copy in copies:
        copy.start()
    return copies


def near_kernel(mine, keep_in, gotten_in, inv_in, other_in, keep, gotten, inv, other, y_ref, sum_ref, sems):
    pairs = [pair_index(2, 0), pair_index(2, 1)]
    moves = [(keep_in, keep), (gotten_in, gotten), (inv_in.at[1], inv.at[1])]
    copies = start_all(sems, moves + [(other_in.at[p], other.at[p]) for p in pairs])
    for copy in copies:
        copy.wait()
    k, _ = place()
    y_ref[k], y_ref[1 - k] = bf16(keep[0]), bf16(gotten[0])
    for t, part in enumerate(lower_part(k, pairs[:1], [y_ref], mine, other, keep, gotten)):
        sum_ref[t] = part


def rest_kernel(keep, gotten, mine, y0, y1, inv_in, other_in, inv, other, sum_ref, sems):
    pairs = [pair_index(3, 0), pair_index(3, 1)]
    order = pairs + [p for p in range(other.shape[0]) if p not in pairs]
    moves = [(other_in.at[p], other.at[p]) for p in order] + [(inv_in.at[i], inv.at[i]) for i in range(inv.shape[0])]
    copies = start_all(sems, moves)
    for copy in copies[:2]:
        copy.wait()
    for t, part in enumerate(lower_part(place()[0], pairs, [y0, y1], mine, other, keep, gotten)):
        sum_ref[t] = part
    for copy in copies[2:]:
        copy.wait()


def ahead_kernel(keep, gotten, mine, other, y0, y1, y2, sum_ref):
    pairs = [pair_index(4, b) for b in range(3)]
    for t, part in enumerate(lower_part(place()[0], pairs, [y0, y1, y2], mine, other, keep, gotten)):
        sum_ref[t] = part


def down_kernel(level, pair, *refs):
    keep, gotten, rhs, rhs_other, inv, inv_other, mine, other, ahead, some, rest = refs[:11]
    y_ref, msg_ref, total_ref = refs[11:]
    k, diagonal = place()
    total_ref[...] = some[...] + rest[...]
    for at, b, inverse in ((k, rhs, inv), (1 - k, rhs_other, inv_other)):
        y_ref[at] = bf16(dot(bf16(f32(b[level]) - total_ref[at]), inverse[level], NT))
    parts = lower_part(k, [pair], [y_ref], mine, other, keep, gotten)
    parts = [ahead[t] + part for t, part in enumerate(parts)]
    if level == 3:
        total_ref[k], total_ref[1 - k] = f32(rhs[4]), f32(rhs_other[4])
        parts = [jnp.where(diagonal, p - total_ref[t], p) for t, p in enumerate(parts)]
    for t, part in enumerate(parts):
        msg_ref[t] = bf16(part)


def up_parts(k, diagonal, level, pairs, solved, y, factors, inv, inv_other):
    parts = upper_part(pairs, solved, *factors)
    outs = []
    for part, at, inverse in zip(parts, (k, 1 - k), (inv, inv_other), strict=True):
        part = jnp.where(diagonal, part - f32(y[at]), part)
        outs.append((at, bf16(dot(bf16(part), inverse[level], NN))))
    return outs


def turn_kernel(n, pairs, *refs):
    keep, gotten, inv_k, inv_o, inv, inv_other, mine, other, y3, own = refs[:10]
    got = refs[10 : 10 + n - 1]
    y_ref, x_ref, msg_ref, whole_k, whole_o = refs[10 + n - 1 :]
    k, diagonal = place()
    low = whole_k.shape[0] // 2
    for packed, inverse in ((inv_k, whole_k), (inv_o, whole_o)):
        inverse[low:, :] = packed[:low]
        inverse[: low // 2, :low] = packed[low:, :low]
        inverse[low // 2 : low, :low] = packed[low:, low:]
        inverse[:low, low:] = jnp.zeros_like(inverse[:low, low:])
    x_ref[...] = bf16(-tree([f32(own[...])] + [f32(g[...]) for g in got]))
    for at, inverse in ((k, whole_k), (1 - k, whole_o)):
        y_ref[at] = bf16(dot(x_ref[at], inverse[...], NT))
    for at, inverse in ((k, whole_k), (1 - k, whole_o)):
        x_ref[at] = bf16(dot(y_ref[at], inverse[...], NN))
    for at, part in up_parts(k, diagonal, 3, pairs, [x_ref], y3, (mine, other, keep, gotten), inv, inv_other):
        msg_ref[at] = part


def up_kernel(level, pairs, *refs):
    keep, gotten, inv, inv_other, mine, other, below, y4, some, rest = refs[:10]
    later = refs[10 : 14 - level]
    outs = refs[14 - level :]
    k, diagonal = place()
    x_ref = outs[0]
    x_ref[...] = bf16(-(some[...] + rest[...]))
    solved = list(later) + [x_ref]
    parts = up_parts(k, diagonal, level - 1, pairs, solved, below, (mine, other, keep, gotten), inv, inv_other)
    if level > 1:
        for at, part in parts:
            outs[1][at] = part
    else:
        for ref, (_, part) in zip(outs[1:], parts, strict=False):
            ref[...] = part
        for i, v in enumerate((y4, *solved)):
            outs[3][i] = v[1 - k]


def out_kernel(n, *refs):
    own, got = refs[0], refs[1:n]
    y, moved = refs[n : n + 4], refs[n + 4]
    forward, solved, forward_ref, solved_ref, sems = refs[n + 5 :]
    k, _ = place()
    for level in range(4):
        forward_ref[level, 0] = y[level][k]
        solved_ref[4 - level, 0] = moved[1 + level]
    forward_ref[4, 0] = moved[0]
    solved_ref[0, 0] = bf16(-tree([f32(own[...])] + [f32(g[...]) for g in got]))
    copies = [
        pltpu.make_async_copy(forward_ref, forward, sems.at[0]),
        pltpu.make_async_copy(solved_ref, solved, sems.at[1]),
    ]
    for copy in copies:
        copy.start()
    for copy in copies:
        copy.wait()


VMEM = pl.BlockSpec(memory_space=pltpu.VMEM)
ANY = pl.BlockSpec(memory_space=pl.ANY)
ROOM = pltpu.CompilerParams(vmem_limit_bytes=16 * 1024 * 1024)


def call(body, outs, args, scratch=(), dtype=jnp.bfloat16):
    return pl.pallas_call(
        body,
        out_shape=[jax.ShapeDtypeStruct(s, dtype) for s in outs],
        in_specs=[VMEM] * len(args),
        out_specs=[VMEM] * len(outs),
        scratch_shapes=list(scratch),
        compiler_params=ROOM,
    )(*args)


def on_device(rhs, factor, pattern, diag_inverse):
    n = lax.axis_size("col")
    levels, own, count, width = rhs.shape
    assert levels == 5 and own == 1 and factor.shape[1] == 2 and lax.axis_size("row") == 2 * n

    rhs, inv = rhs[:, 0], diag_inverse[:, 0]
    mine = factor[:, :, 0]
    swap = functools.partial(lax.ppermute, axis_name=BOTH, perm=core_perm(n))
    send = lambda x, perms: [lax.ppermute(x, BOTH, p) for p in perms]
    vec, slots = (2, count, width), (4, count, width)

    def share(msg, perms):
        got = send(msg, perms)
        some = tree([f32(g) for g in got])
        return got, some, swap(some)

    first = lambda x, at: pl.BlockSpec((1, *x.shape[1:]), lambda i: (at,) + (0,) * (len(x.shape) - 1))
    keep, give, last = pl.pallas_call(
        start_kernel,
        grid=(1,),
        out_shape=[jax.ShapeDtypeStruct(slots, jnp.float32)] * 2 + [jax.ShapeDtypeStruct((3 * width // 4, width), inv.dtype)],
        in_specs=[pl.BlockSpec(memory_space=pltpu.SMEM), first(rhs, 0), first(inv, 0), first(inv, 4), first(mine, 0)],
        out_specs=[VMEM] * 3,
        compiler_params=pltpu.CompilerParams(vmem_limit_bytes=61 * 1024 * 1024),
    )(pattern.transpose(1, 2, 0), rhs, inv, inv, mine)
    gotten = swap(give)
    inv_s, mine_s, rhs_s, _ = lax.optimization_barrier((inv, mine, rhs, gotten))
    inv_o, other, rhs_o = swap(inv_s), swap(mine_s), swap(rhs_s)
    inv_to = lax.ppermute(last, BOTH, far_perm(n))

    y = [None] * 5
    x = [None] * 5
    msg = bf16(keep[1:3] + gotten[1:3])
    for level in range(1, 4):
        got, some, rest = share(msg, down_perms(n))
        early, solved, _ = lax.optimization_barrier(((inv_o, other), y[:level], got[0]))
        if level == 1:
            inv_near, other_near = early
            keep, gotten, inv_near, other_near, y[0], ahead = pl.pallas_call(
                near_kernel,
                out_shape=[jax.ShapeDtypeStruct(a.shape, a.dtype) for a in (keep, gotten, inv_o, other)]
                + [jax.ShapeDtypeStruct(vec, jnp.bfloat16), jax.ShapeDtypeStruct(vec, jnp.float32)],
                in_specs=[VMEM] + [ANY] * 4,
                out_specs=[VMEM] * 6,
                scratch_shapes=[pltpu.SemaphoreType.DMA((5,))],
                compiler_params=ROOM,
            )(mine, keep, gotten, *early)
            held = inv_near, other_near
        elif level == 2:
            *held, ahead = pl.pallas_call(
                rest_kernel,
                out_shape=[jax.ShapeDtypeStruct(a.shape, a.dtype) for a in (inv_o, other)]
                + [jax.ShapeDtypeStruct(vec, jnp.float32)],
                in_specs=[VMEM] * 5 + [ANY] * 2,
                out_specs=[VMEM] * 3,
                scratch_shapes=[pltpu.SemaphoreType.DMA((inv_o.shape[0] + other.shape[0],))],
                compiler_params=ROOM,
            )(keep, gotten, mine, *solved, *early)
            inv_o, other = held
        else:
            (ahead,) = call(ahead_kernel, [vec], (keep, gotten, mine, other, *solved), dtype=jnp.float32)
        y[level], msg = call(
            functools.partial(down_kernel, level, pair_index(level + 1, level)),
            [vec, vec],
            (keep, gotten, rhs, rhs_o, inv, held[0], mine, held[1], ahead, some, rest),
            [pltpu.VMEM(vec, jnp.float32)],
        )
        if level == 1:
            msg, inv_to = lax.optimization_barrier((msg, inv_to))
            inv_tk = swap(inv_to)
    got = send(msg, plane_perms(n))
    y[4], x[4], msg = call(
        functools.partial(turn_kernel, n, [pair_index(4, 3)]),
        [vec, vec, vec],
        (keep, gotten, inv_tk, inv_to, inv, inv_o, mine, other, y[3], msg, *got),
        [pltpu.VMEM((width, width), inv.dtype)] * 2,
    )
    for level in (3, 2, 1):
        got, some, rest = share(msg, up_perms(n))
        pairs = [pair_index(c, level - 1) for c in range(4, level - 1, -1)]
        x[level], msg, *more = call(
            functools.partial(up_kernel, level, pairs),
            [vec, vec] if level > 1 else [vec, vec[1:], vec[1:], (5, *vec[1:])],
            (keep, gotten, inv, inv_o, mine, other, y[level - 1], y[4], some, rest, *x[4:level:-1]),
        )
    moved = lax.ppermute(more[1], BOTH, turn_perm(n))
    got = [lax.ppermute(more[0] if m & 1 else msg, BOTH, p) for m, p in enumerate(line_perms(n), 1)]
    out = jax.ShapeDtypeStruct((levels, 1, count, width), jnp.bfloat16)
    return pl.pallas_call(
        functools.partial(out_kernel, n),
        out_shape=[out, out],
        in_specs=[VMEM] * (n + 5),
        out_specs=[ANY] * 2,
        scratch_shapes=[pltpu.VMEM(out.shape, out.dtype)] * 2 + [pltpu.SemaphoreType.DMA((2,))],
        compiler_params=ROOM,
    )(msg, *got, *y[:4], moved)


def solution(mesh):
    return jax.shard_map(
        on_device,
        mesh=mesh,
        in_specs=(
            P(None, "row", None, None),
            P(None, "col", "row", None, None),
            P(None, "col", "row"),
            P(None, "row", None, None),
        ),
        out_specs=(P(None, "row", None, None), P(None, "row", None, None)),
        check_vma=False,
    )
```

```python
import functools

import jax
import jax.numpy as jnp
from jax import lax
from jax.experimental import pallas as pl
from jax.experimental.pallas import tpu as pltpu
from jax.sharding import PartitionSpec as P

BOTH = ("row", "col")
NT = (((1,), (1,)), ((), ()))
NN = (((1,), (0,)), ((), ()))


def pair_index(later, earlier):
    return later * (later - 1) // 2 + earlier


def perm(n, target):
    pairs = []
    for q in range(n):
        for k in range(2):
            for z in range(n):
                a, b, c = target(q, k, z)
                assert (a, b, c) != (q, k, z)
                pairs.append(((2 * q + k) * n + z, (2 * a + b) * n + c))
    return pairs


def down_perms(n):
    return [perm(n, lambda q, k, z, j=j: (z, (q & 1) ^ 1, 2 * ((q >> 1) ^ j) + k)) for j in range(n // 2)]


def up_perms(n):
    return [perm(n, lambda q, k, z, j=j: (2 * ((z >> 1) ^ j) + k, (z & 1) ^ 1, q)) for j in reversed(range(n // 2))]


def plane_perms(n):
    return [perm(n, lambda q, k, z, m=m: (q ^ m, k ^ 1, z)) for m in range(1, n)]


def line_perms(n):
    return [perm(n, lambda q, k, z, m=m: (q, k ^ 1, z ^ m)) for m in range(1, n)]


def turn_perm(n):
    return perm(n, lambda q, k, z: (z, k ^ 1, q ^ (n - 1)))


def far_perm(n):
    return perm(n, lambda q, k, z: (z ^ (n - 1), k ^ 1, q))


def core_perm(n):
    return perm(n, lambda q, k, z: (q, k ^ 1, z))


def tree(parts):
    while len(parts) > 1:
        half = len(parts) // 2
        parts = [parts[i] + parts[i + half] for i in range(half)]
    return parts[0]


def f32(x):
    return x.astype(jnp.float32)


def bf16(x):
    return x.astype(jnp.bfloat16)


def dot(a, b, dims):
    return lax.dot_general(a, b, dims, preferred_element_type=jnp.float32)


def place():
    row = lax.axis_index("row")
    return row % 2, row // 2 == lax.axis_index("col")


def row_of(mask, p, t):
    return mask[3, pl.ds(2 * p + t, 1), :]


def lower_part(k, pairs, solved, mine, other, keep, gotten):
    outs = []
    for t in range(2):
        acc = None
        for p, y in zip(pairs, solved, strict=True):
            a = dot(y[k], mine[p, t], NT) * row_of(keep, p, t)
            b = dot(y[1 - k], other[p, t], NT) * row_of(gotten, p, t)
            acc = a + b if acc is None else acc + (a + b)
        outs.append(acc)
    return outs


def upper_part(pairs, solved, mine, other, keep, gotten):
    outs = []
    for blocks, mask in ((mine, keep), (other, gotten)):
        acc = None
        for p, x in zip(pairs, solved, strict=True):
            for t in range(2):
                a = dot(x[t], blocks[p, t], NN) * row_of(mask, p, t)
                acc = a if acc is None else acc + a
        outs.append(acc)
    return outs


def start_kernel(pattern, rhs, inv, last, mine, keep_ref, give_ref, last_ref):
    low = last.shape[1] // 2
    last_ref[:low] = last[0, low:, :]
    last_ref[low:, :low] = last[0, : low // 2, :low]
    last_ref[low:, low:] = last[0, low // 2 : low, :low]
    y = bf16(dot(rhs[0], inv[0], NT))
    keep_ref[0] = f32(y)
    for t in range(2):
        keep_ref[1 + t] = dot(y, mine[0, t], NT) * f32(pattern[t, 0, 0])
    for i in range(keep_ref.shape[1]):
        value = f32(pattern[i % 2, 0, i // 2]) if i < 2 * pattern.shape[2] else 0.0
        keep_ref[3, pl.ds(i, 1), :] = jnp.full((1, keep_ref.shape[2]), value, jnp.float32)
    give_ref[...] = keep_ref[...]


def start_all(sems, moves):
    copies = [pltpu.make_async_copy(a, b, sems.at[i]) for i, (a, b) in enumerate(moves)]
    for copy in copies:
        copy.start()
    return copies


def near_kernel(mine, keep_in, gotten_in, inv_in, other_in, keep, gotten, inv, other, y_ref, sum_ref, sems):
    pairs = [pair_index(2, 0), pair_index(2, 1)]
    moves = [(keep_in, keep), (gotten_in, gotten), (inv_in.at[1], inv.at[1])]
    copies = start_all(sems, moves + [(other_in.at[p], other.at[p]) for p in pairs])
    for copy in copies:
        copy.wait()
    k, _ = place()
    y_ref[k], y_ref[1 - k] = bf16(keep[0]), bf16(gotten[0])
    for t, part in enumerate(lower_part(k, pairs[:1], [y_ref], mine, other, keep, gotten)):
        sum_ref[t] = part


def rest_kernel(keep, gotten, mine, y0, y1, inv_in, other_in, inv, other, sum_ref, sems):
    pairs = [pair_index(3, 0), pair_index(3, 1)]
    order = pairs + [p for p in range(other.shape[0]) if p not in pairs]
    moves = [(other_in.at[p], other.at[p]) for p in order] + [(inv_in.at[i], inv.at[i]) for i in range(inv.shape[0])]
    copies = start_all(sems, moves)
    for copy in copies[:2]:
        copy.wait()
    for t, part in enumerate(lower_part(place()[0], pairs, [y0, y1], mine, other, keep, gotten)):
        sum_ref[t] = part
    for copy in copies[2:]:
        copy.wait()


def ahead_kernel(keep, gotten, mine, other, y0, y1, y2, sum_ref):
    pairs = [pair_index(4, b) for b in range(3)]
    for t, part in enumerate(lower_part(place()[0], pairs, [y0, y1, y2], mine, other, keep, gotten)):
        sum_ref[t] = part


def down_kernel(level, pair, *refs):
    keep, gotten, rhs, rhs_other, inv, inv_other, mine, other, ahead, some, rest = refs[:11]
    y_ref, msg_ref, total_ref = refs[11:]
    k, diagonal = place()
    total_ref[...] = some[...] + rest[...]
    for at, b, inverse in ((k, rhs, inv), (1 - k, rhs_other, inv_other)):
        y_ref[at] = bf16(dot(bf16(f32(b[level]) - total_ref[at]), inverse[level], NT))
    parts = lower_part(k, [pair], [y_ref], mine, other, keep, gotten)
    parts = [ahead[t] + part for t, part in enumerate(parts)]
    if level == 3:
        total_ref[k], total_ref[1 - k] = f32(rhs[4]), f32(rhs_other[4])
        parts = [jnp.where(diagonal, p - total_ref[t], p) for t, p in enumerate(parts)]
    for t, part in enumerate(parts):
        msg_ref[t] = bf16(part)


def above_kernel(pairs, *refs):
    keep, gotten, mine, other = refs[:4]
    for i, part in enumerate(upper_part(pairs, refs[4:-1], mine, other, keep, gotten)):
        refs[-1][i] = part


def up_parts(k, diagonal, level, pairs, solved, y, factors, inv, inv_other, ahead=None):
    parts = upper_part(pairs, solved, *factors)
    if ahead is not None:
        parts = [ahead[i] + part for i, part in enumerate(parts)]
    outs = []
    for part, at, inverse in zip(parts, (k, 1 - k), (inv, inv_other), strict=True):
        part = jnp.where(diagonal, part - f32(y[at]), part)
        outs.append((at, bf16(dot(bf16(part), inverse[level], NN))))
    return outs


def turn_kernel(n, pairs, *refs):
    keep, gotten, inv_k, inv_o, inv, inv_other, mine, other, y3, own = refs[:10]
    got = refs[10 : 10 + n - 1]
    y_ref, x_ref, msg_ref, whole_k, whole_o = refs[10 + n - 1 :]
    k, diagonal = place()
    low = whole_k.shape[0] // 2
    for packed, inverse in ((inv_k, whole_k), (inv_o, whole_o)):
        inverse[low:, :] = packed[:low]
        inverse[: low // 2, :low] = packed[low:, :low]
        inverse[low // 2 : low, :low] = packed[low:, low:]
        inverse[:low, low:] = jnp.zeros_like(inverse[:low, low:])
    x_ref[...] = bf16(-tree([f32(own[...])] + [f32(g[...]) for g in got]))
    for at, inverse in ((k, whole_k), (1 - k, whole_o)):
        y_ref[at] = bf16(dot(x_ref[at], inverse[...], NT))
    for at, inverse in ((k, whole_k), (1 - k, whole_o)):
        x_ref[at] = bf16(dot(y_ref[at], inverse[...], NN))
    for at, part in up_parts(k, diagonal, 3, pairs, [x_ref], y3, (mine, other, keep, gotten), inv, inv_other):
        msg_ref[at] = part


def up_kernel(level, pairs, *refs):
    keep, gotten, inv, inv_other, mine, other, below, y4, some, rest, ahead = refs[:11]
    later = refs[11 : 15 - level]
    outs = refs[15 - level :]
    k, diagonal = place()
    x_ref = outs[0]
    x_ref[...] = bf16(-(some[...] + rest[...]))
    solved = list(later) + [x_ref]
    factors = (mine, other, keep, gotten)
    parts = up_parts(k, diagonal, level - 1, pairs, [x_ref], below, factors, inv, inv_other, ahead)
    if level > 1:
        for at, part in parts:
            outs[1][at] = part
    else:
        for ref, (_, part) in zip(outs[1:], parts, strict=False):
            ref[...] = part
        for i, v in enumerate((y4, *solved)):
            outs[3][i] = v[1 - k]


def out_kernel(n, *refs):
    own, got = refs[0], refs[1:n]
    y, moved = refs[n : n + 4], refs[n + 4]
    forward, solved, forward_ref, solved_ref, sems = refs[n + 5 :]
    k, _ = place()
    for level in range(4):
        forward_ref[level, 0] = y[level][k]
        solved_ref[4 - level, 0] = moved[1 + level]
    forward_ref[4, 0] = moved[0]
    solved_ref[0, 0] = bf16(-tree([f32(own[...])] + [f32(g[...]) for g in got]))
    copies = [
        pltpu.make_async_copy(forward_ref, forward, sems.at[0]),
        pltpu.make_async_copy(solved_ref, solved, sems.at[1]),
    ]
    for copy in copies:
        copy.start()
    for copy in copies:
        copy.wait()


VMEM = pl.BlockSpec(memory_space=pltpu.VMEM)
ANY = pl.BlockSpec(memory_space=pl.ANY)
ROOM = pltpu.CompilerParams(vmem_limit_bytes=16 * 1024 * 1024)


def call(body, outs, args, scratch=(), dtype=jnp.bfloat16):
    return pl.pallas_call(
        body,
        out_shape=[jax.ShapeDtypeStruct(s, dtype) for s in outs],
        in_specs=[VMEM] * len(args),
        out_specs=[VMEM] * len(outs),
        scratch_shapes=list(scratch),
        compiler_params=ROOM,
    )(*args)


def on_device(rhs, factor, pattern, diag_inverse):
    n = lax.axis_size("col")
    levels, own, count, width = rhs.shape
    assert levels == 5 and own == 1 and factor.shape[1] == 2 and lax.axis_size("row") == 2 * n

    rhs, inv = rhs[:, 0], diag_inverse[:, 0]
    mine = factor[:, :, 0]
    swap = functools.partial(lax.ppermute, axis_name=BOTH, perm=core_perm(n))
    send = lambda x, perms: [lax.ppermute(x, BOTH, p) for p in perms]
    vec, slots = (2, count, width), (4, count, width)

    def share(msg, perms):
        got = send(msg, perms)
        some = tree([f32(g) for g in got])
        return got, some, swap(some)

    first = lambda x, at: pl.BlockSpec((1, *x.shape[1:]), lambda i: (at,) + (0,) * (len(x.shape) - 1))
    keep, give, last = pl.pallas_call(
        start_kernel,
        grid=(1,),
        out_shape=[jax.ShapeDtypeStruct(slots, jnp.float32)] * 2 + [jax.ShapeDtypeStruct((3 * width // 4, width), inv.dtype)],
        in_specs=[pl.BlockSpec(memory_space=pltpu.SMEM), first(rhs, 0), first(inv, 0), first(inv, 4), first(mine, 0)],
        out_specs=[VMEM] * 3,
        compiler_params=pltpu.CompilerParams(vmem_limit_bytes=61 * 1024 * 1024),
    )(pattern.transpose(1, 2, 0), rhs, inv, inv, mine)
    gotten = swap(give)
    msg = bf16(keep[1:3] + gotten[1:3])
    inv_s, mine_s, rhs_s, _ = lax.optimization_barrier((inv, mine, rhs, msg))
    inv_o, other, rhs_o = swap(inv_s), swap(mine_s), swap(rhs_s)
    inv_to = lax.ppermute(last, BOTH, far_perm(n))

    y = [None] * 5
    x = [None] * 5
    for level in range(1, 4):
        got, some, rest = share(msg, down_perms(n))
        early, solved, _ = lax.optimization_barrier(((inv_o, other), y[:level], got[0]))
        if level == 1:
            inv_near, other_near = early
            keep, gotten, inv_near, other_near, y[0], ahead = pl.pallas_call(
                near_kernel,
                out_shape=[jax.ShapeDtypeStruct(a.shape, a.dtype) for a in (keep, gotten, inv_o, other)]
                + [jax.ShapeDtypeStruct(vec, jnp.bfloat16), jax.ShapeDtypeStruct(vec, jnp.float32)],
                in_specs=[VMEM] + [ANY] * 4,
                out_specs=[VMEM] * 6,
                scratch_shapes=[pltpu.SemaphoreType.DMA((5,))],
                compiler_params=ROOM,
            )(mine, keep, gotten, *early)
            held = inv_near, other_near
        elif level == 2:
            *held, ahead = pl.pallas_call(
                rest_kernel,
                out_shape=[jax.ShapeDtypeStruct(a.shape, a.dtype) for a in (inv_o, other)]
                + [jax.ShapeDtypeStruct(vec, jnp.float32)],
                in_specs=[VMEM] * 5 + [ANY] * 2,
                out_specs=[VMEM] * 3,
                scratch_shapes=[pltpu.SemaphoreType.DMA((inv_o.shape[0] + other.shape[0],))],
                compiler_params=ROOM,
            )(keep, gotten, mine, *solved, *early)
            inv_o, other = held
        else:
            (ahead,) = call(ahead_kernel, [vec], (keep, gotten, mine, other, *solved), dtype=jnp.float32)
        y[level], msg = call(
            functools.partial(down_kernel, level, pair_index(level + 1, level)),
            [vec, vec],
            (keep, gotten, rhs, rhs_o, inv, held[0], mine, held[1], ahead, some, rest),
            [pltpu.VMEM(vec, jnp.float32)],
        )
        if level == 1:
            msg, inv_to = lax.optimization_barrier((msg, inv_to))
            inv_tk = swap(inv_to)
    got = send(msg, plane_perms(n))
    y[4], x[4], msg = call(
        functools.partial(turn_kernel, n, [pair_index(4, 3)]),
        [vec, vec, vec],
        (keep, gotten, inv_tk, inv_to, inv, inv_o, mine, other, y[3], msg, *got),
        [pltpu.VMEM((width, width), inv.dtype)] * 2,
    )
    for level in (3, 2, 1):
        got, some, rest = share(msg, up_perms(n))
        later, _ = lax.optimization_barrier((x[4:level:-1], got[0]))
        pairs = [pair_index(c, level - 1) for c in range(4, level, -1)]
        (ahead,) = call(
            functools.partial(above_kernel, pairs), [vec], (keep, gotten, mine, other, *later), dtype=jnp.float32
        )
        pairs = [pair_index(level, level - 1)]
        x[level], msg, *more = call(
            functools.partial(up_kernel, level, pairs),
            [vec, vec] if level > 1 else [vec, vec[1:], vec[1:], (5, *vec[1:])],
            (keep, gotten, inv, inv_o, mine, other, y[level - 1], y[4], some, rest, ahead, *x[4:level:-1]),
        )
    moved = lax.ppermute(more[1], BOTH, turn_perm(n))
    lines = line_perms(n)
    order = sorted(range(1, n), key=lambda m: (m & (m + 1) != 0, m))
    got = {m: lax.ppermute(more[0], BOTH, lines[m - 1]) for m in order}
    got = [got[m] for m in range(1, n)]
    out = jax.ShapeDtypeStruct((levels, 1, count, width), jnp.bfloat16)
    return pl.pallas_call(
        functools.partial(out_kernel, n),
        out_shape=[out, out],
        in_specs=[VMEM] * (n + 5),
        out_specs=[ANY] * 2,
        scratch_shapes=[pltpu.VMEM(out.shape, out.dtype)] * 2 + [pltpu.SemaphoreType.DMA((2,))],
        compiler_params=ROOM,
    )(msg, *got, *y[:4], moved)


def solution(mesh):
    return jax.shard_map(
        on_device,
        mesh=mesh,
        in_specs=(
            P(None, "row", None, None),
            P(None, "col", "row", None, None),
            P(None, "col", "row"),
            P(None, "row", None, None),
        ),
        out_specs=(P(None, "row", None, None), P(None, "row", None, None)),
        check_vma=False,
    )
```

```python
import functools

import jax
import jax.numpy as jnp
from jax import lax
from jax.experimental import pallas as pl
from jax.experimental.pallas import tpu as pltpu
from jax.sharding import PartitionSpec as P

BOTH = ("row", "col")
NT = (((1,), (1,)), ((), ()))
NN = (((1,), (0,)), ((), ()))


def pair_index(later, earlier):
    return later * (later - 1) // 2 + earlier


def perm(n, target):
    pairs = []
    for q in range(n):
        for k in range(2):
            for z in range(n):
                a, b, c = target(q, k, z)
                assert (a, b, c) != (q, k, z)
                pairs.append(((2 * q + k) * n + z, (2 * a + b) * n + c))
    return pairs


def down_perms(n):
    return [perm(n, lambda q, k, z, j=j: (z, (q & 1) ^ 1, 2 * ((q >> 1) ^ j) + k)) for j in range(n // 2)]


def up_perms(n):
    return [perm(n, lambda q, k, z, j=j: (2 * ((z >> 1) ^ j) + k, (z & 1) ^ 1, q)) for j in reversed(range(n // 2))]


def plane_perms(n):
    return [perm(n, lambda q, k, z, m=m: (q ^ m, k ^ 1, z)) for m in range(1, n)]


def line_perms(n):
    return [perm(n, lambda q, k, z, m=m: (q, k ^ 1, z ^ m)) for m in range(1, n)]


def turn_perm(n):
    return perm(n, lambda q, k, z: (z, k ^ 1, q ^ (n - 1)))


def far_perm(n):
    return perm(n, lambda q, k, z: (z ^ (n - 1), k ^ 1, q))


def core_perm(n):
    return perm(n, lambda q, k, z: (q, k ^ 1, z))


def tree(parts):
    while len(parts) > 1:
        half = len(parts) // 2
        parts = [parts[i] + parts[i + half] for i in range(half)]
    return parts[0]


def f32(x):
    return x.astype(jnp.float32)


def bf16(x):
    return x.astype(jnp.bfloat16)


def dot(a, b, dims):
    return lax.dot_general(a, b, dims, preferred_element_type=jnp.float32)


def place():
    row = lax.axis_index("row")
    return row % 2, row // 2 == lax.axis_index("col")


def row_of(mask, p, t):
    return mask[3, pl.ds(2 * p + t, 1), :]


def lower_part(k, pairs, solved, mine, other, keep, gotten):
    outs = []
    for t in range(2):
        acc = None
        for p, y in zip(pairs, solved, strict=True):
            a = dot(y[k], mine[p, t], NT) * row_of(keep, p, t)
            b = dot(y[1 - k], other[p, t], NT) * row_of(gotten, p, t)
            acc = a + b if acc is None else acc + (a + b)
        outs.append(acc)
    return outs


def upper_part(pairs, solved, mine, other, keep, gotten):
    outs = []
    for blocks, mask in ((mine, keep), (other, gotten)):
        acc = None
        for p, x in zip(pairs, solved, strict=True):
            for t in range(2):
                a = dot(x[t], blocks[p, t], NN) * row_of(mask, p, t)
                acc = a if acc is None else acc + a
        outs.append(acc)
    return outs


def start_kernel(pattern, rhs, inv, last, mine, keep_ref, give_ref, last_ref):
    low = last.shape[1] // 2
    last_ref[:low] = last[0, low:, :]
    last_ref[low:, :low] = last[0, : low // 2, :low]
    last_ref[low:, low:] = last[0, low // 2 : low, :low]
    y = bf16(dot(rhs[0], inv[0], NT))
    keep_ref[0] = f32(y)
    for t in range(2):
        keep_ref[1 + t] = dot(y, mine[0, t], NT) * f32(pattern[t, 0, 0])
    for i in range(keep_ref.shape[1]):
        value = f32(pattern[i % 2, 0, i // 2]) if i < 2 * pattern.shape[2] else 0.0
        keep_ref[3, pl.ds(i, 1), :] = jnp.full((1, keep_ref.shape[2]), value, jnp.float32)
    give_ref[...] = keep_ref[...]


def start_all(sems, moves):
    copies = [pltpu.make_async_copy(a, b, sems.at[i]) for i, (a, b) in enumerate(moves)]
    for copy in copies:
        copy.start()
    return copies


def near_kernel(mine, keep_in, gotten_in, inv_in, other_in, keep, gotten, inv, other, y_ref, sum_ref, sems):
    pairs = [pair_index(2, 0), pair_index(2, 1)]
    moves = [(keep_in, keep), (gotten_in, gotten), (inv_in.at[1], inv.at[1])]
    copies = start_all(sems, moves + [(other_in.at[p], other.at[p]) for p in pairs])
    for copy in copies:
        copy.wait()
    k, _ = place()
    y_ref[k], y_ref[1 - k] = bf16(keep[0]), bf16(gotten[0])
    for t, part in enumerate(lower_part(k, pairs[:1], [y_ref], mine, other, keep, gotten)):
        sum_ref[t] = part


def rest_kernel(keep, gotten, mine, y0, y1, inv_in, other_in, inv, other, sum_ref, sems):
    pairs = [pair_index(3, 0), pair_index(3, 1)]
    order = pairs + [p for p in range(other.shape[0]) if p not in pairs]
    moves = [(other_in.at[p], other.at[p]) for p in order] + [(inv_in.at[i], inv.at[i]) for i in range(inv.shape[0])]
    copies = start_all(sems, moves)
    for copy in copies[:2]:
        copy.wait()
    for t, part in enumerate(lower_part(place()[0], pairs, [y0, y1], mine, other, keep, gotten)):
        sum_ref[t] = part
    for copy in copies[2:]:
        copy.wait()


def ahead_kernel(keep, gotten, mine, other, y0, y1, y2, sum_ref):
    pairs = [pair_index(4, b) for b in range(3)]
    for t, part in enumerate(lower_part(place()[0], pairs, [y0, y1, y2], mine, other, keep, gotten)):
        sum_ref[t] = part


def down_kernel(level, pair, *refs):
    keep, gotten, rhs, rhs_other, inv, inv_other, mine, other, ahead, some, rest = refs[:11]
    y_ref, msg_ref, total_ref = refs[11:]
    k, diagonal = place()
    total_ref[...] = f32(some[...]) + f32(rest[...])
    for at, b, inverse in ((k, rhs, inv), (1 - k, rhs_other, inv_other)):
        y_ref[at] = bf16(dot(bf16(f32(b[level]) - total_ref[at]), inverse[level], NT))
    parts = lower_part(k, [pair], [y_ref], mine, other, keep, gotten)
    parts = [ahead[t] + part for t, part in enumerate(parts)]
    if level == 3:
        total_ref[k], total_ref[1 - k] = f32(rhs[4]), f32(rhs_other[4])
        parts = [jnp.where(diagonal, p - total_ref[t], p) for t, p in enumerate(parts)]
    for t, part in enumerate(parts):
        msg_ref[t] = bf16(part)


def above_kernel(pairs, *refs):
    keep, gotten, mine, other = refs[:4]
    for i, part in enumerate(upper_part(pairs, refs[4:-1], mine, other, keep, gotten)):
        refs[-1][i] = part


def up_parts(k, diagonal, level, pairs, solved, y, factors, inv, inv_other, ahead=None):
    parts = upper_part(pairs, solved, *factors)
    if ahead is not None:
        parts = [ahead[i] + part for i, part in enumerate(parts)]
    outs = []
    for part, at, inverse in zip(parts, (k, 1 - k), (inv, inv_other), strict=True):
        part = jnp.where(diagonal, part - f32(y[at]), part)
        outs.append((at, bf16(dot(bf16(part), inverse[level], NN))))
    return outs


def turn_kernel(n, pairs, *refs):
    keep, gotten, inv_k, inv_o, inv, inv_other, mine, other, y3, own = refs[:10]
    got = refs[10 : 10 + n - 1]
    y_ref, x_ref, msg_ref, whole_k, whole_o = refs[10 + n - 1 :]
    k, diagonal = place()
    low = whole_k.shape[0] // 2
    for packed, inverse in ((inv_k, whole_k), (inv_o, whole_o)):
        inverse[low:, :] = packed[:low]
        inverse[: low // 2, :low] = packed[low:, :low]
        inverse[low // 2 : low, :low] = packed[low:, low:]
        inverse[:low, low:] = jnp.zeros_like(inverse[:low, low:])
    x_ref[...] = bf16(-tree([f32(own[...])] + [f32(g[...]) for g in got]))
    for at, inverse in ((k, whole_k), (1 - k, whole_o)):
        y_ref[at] = bf16(dot(x_ref[at], inverse[...], NT))
    for at, inverse in ((k, whole_k), (1 - k, whole_o)):
        x_ref[at] = bf16(dot(y_ref[at], inverse[...], NN))
    for at, part in up_parts(k, diagonal, 3, pairs, [x_ref], y3, (mine, other, keep, gotten), inv, inv_other):
        msg_ref[at] = part


def up_kernel(level, pairs, *refs):
    keep, gotten, inv, inv_other, mine, other, below, y4, some, rest, ahead = refs[:11]
    later = refs[11 : 15 - level]
    outs = refs[15 - level :]
    k, diagonal = place()
    x_ref = outs[0]
    x_ref[...] = bf16(-(f32(some[...]) + f32(rest[...])))
    solved = list(later) + [x_ref]
    factors = (mine, other, keep, gotten)
    parts = up_parts(k, diagonal, level - 1, pairs, [x_ref], below, factors, inv, inv_other, ahead)
    if level > 1:
        for at, part in parts:
            outs[1][at] = part
    else:
        for ref, (_, part) in zip(outs[1:], parts, strict=False):
            ref[...] = part
        for i, v in enumerate((y4, *solved)):
            outs[3][i] = v[1 - k]


def out_kernel(n, *refs):
    own, got = refs[0], refs[1:n]
    y, moved = refs[n : n + 4], refs[n + 4]
    forward, solved, forward_ref, solved_ref, sems = refs[n + 5 :]
    k, _ = place()
    for level in range(4):
        forward_ref[level, 0] = y[level][k]
        solved_ref[4 - level, 0] = moved[1 + level]
    forward_ref[4, 0] = moved[0]
    solved_ref[0, 0] = bf16(-tree([f32(own[...])] + [f32(g[...]) for g in got]))
    copies = [
        pltpu.make_async_copy(forward_ref, forward, sems.at[0]),
        pltpu.make_async_copy(solved_ref, solved, sems.at[1]),
    ]
    for copy in copies:
        copy.start()
    for copy in copies:
        copy.wait()


VMEM = pl.BlockSpec(memory_space=pltpu.VMEM)
ANY = pl.BlockSpec(memory_space=pl.ANY)
ROOM = pltpu.CompilerParams(vmem_limit_bytes=16 * 1024 * 1024)


def call(body, outs, args, scratch=(), dtype=jnp.bfloat16):
    return pl.pallas_call(
        body,
        out_shape=[jax.ShapeDtypeStruct(s, dtype) for s in outs],
        in_specs=[VMEM] * len(args),
        out_specs=[VMEM] * len(outs),
        scratch_shapes=list(scratch),
        compiler_params=ROOM,
    )(*args)


def on_device(rhs, factor, pattern, diag_inverse):
    n = lax.axis_size("col")
    levels, own, count, width = rhs.shape
    assert levels == 5 and own == 1 and factor.shape[1] == 2 and lax.axis_size("row") == 2 * n

    rhs, inv = rhs[:, 0], diag_inverse[:, 0]
    mine = factor[:, :, 0]
    swap = functools.partial(lax.ppermute, axis_name=BOTH, perm=core_perm(n))
    send = lambda x, perms: [lax.ppermute(x, BOTH, p) for p in perms]
    vec, slots = (2, count, width), (4, count, width)

    def share(msg, perms):
        got = send(msg, perms)
        some = bf16(tree([f32(g) for g in got]))
        return got, some, swap(some)

    first = lambda x, at: pl.BlockSpec((1, *x.shape[1:]), lambda i: (at,) + (0,) * (len(x.shape) - 1))
    keep, give, last = pl.pallas_call(
        start_kernel,
        grid=(1,),
        out_shape=[jax.ShapeDtypeStruct(slots, jnp.float32)] * 2 + [jax.ShapeDtypeStruct((3 * width // 4, width), inv.dtype)],
        in_specs=[pl.BlockSpec(memory_space=pltpu.SMEM), first(rhs, 0), first(inv, 0), first(inv, 4), first(mine, 0)],
        out_specs=[VMEM] * 3,
        compiler_params=pltpu.CompilerParams(vmem_limit_bytes=61 * 1024 * 1024),
    )(pattern.transpose(1, 2, 0), rhs, inv, inv, mine)
    gotten = swap(give)
    msg = bf16(keep[1:3] + gotten[1:3])
    inv_s, mine_s, rhs_s, _ = lax.optimization_barrier((inv, mine, rhs, msg))
    inv_o, other, rhs_o = swap(inv_s), swap(mine_s), swap(rhs_s)
    inv_to = lax.ppermute(last, BOTH, far_perm(n))

    y = [None] * 5
    x = [None] * 5
    for level in range(1, 4):
        got, some, rest = share(msg, down_perms(n))
        early, solved, _ = lax.optimization_barrier(((inv_o, other), y[:level], got[0]))
        if level == 1:
            inv_near, other_near = early
            keep, gotten, inv_near, other_near, y[0], ahead = pl.pallas_call(
                near_kernel,
                out_shape=[jax.ShapeDtypeStruct(a.shape, a.dtype) for a in (keep, gotten, inv_o, other)]
                + [jax.ShapeDtypeStruct(vec, jnp.bfloat16), jax.ShapeDtypeStruct(vec, jnp.float32)],
                in_specs=[VMEM] + [ANY] * 4,
                out_specs=[VMEM] * 6,
                scratch_shapes=[pltpu.SemaphoreType.DMA((5,))],
                compiler_params=ROOM,
            )(mine, keep, gotten, *early)
            held = inv_near, other_near
        elif level == 2:
            *held, ahead = pl.pallas_call(
                rest_kernel,
                out_shape=[jax.ShapeDtypeStruct(a.shape, a.dtype) for a in (inv_o, other)]
                + [jax.ShapeDtypeStruct(vec, jnp.float32)],
                in_specs=[VMEM] * 5 + [ANY] * 2,
                out_specs=[VMEM] * 3,
                scratch_shapes=[pltpu.SemaphoreType.DMA((inv_o.shape[0] + other.shape[0],))],
                compiler_params=ROOM,
            )(keep, gotten, mine, *solved, *early)
            inv_o, other = held
        else:
            (ahead,) = call(ahead_kernel, [vec], (keep, gotten, mine, other, *solved), dtype=jnp.float32)
        y[level], msg = call(
            functools.partial(down_kernel, level, pair_index(level + 1, level)),
            [vec, vec],
            (keep, gotten, rhs, rhs_o, inv, held[0], mine, held[1], ahead, some, rest),
            [pltpu.VMEM(vec, jnp.float32)],
        )
        if level == 1:
            msg, inv_to = lax.optimization_barrier((msg, inv_to))
            inv_tk = swap(inv_to)
    got = send(msg, plane_perms(n))
    y[4], x[4], msg = call(
        functools.partial(turn_kernel, n, [pair_index(4, 3)]),
        [vec, vec, vec],
        (keep, gotten, inv_tk, inv_to, inv, inv_o, mine, other, y[3], msg, *got),
        [pltpu.VMEM((width, width), inv.dtype)] * 2,
    )
    for level in (3, 2, 1):
        got, some, rest = share(msg, up_perms(n))
        later, _ = lax.optimization_barrier((x[4:level:-1], got[0]))
        pairs = [pair_index(c, level - 1) for c in range(4, level, -1)]
        (ahead,) = call(
            functools.partial(above_kernel, pairs), [vec], (keep, gotten, mine, other, *later), dtype=jnp.float32
        )
        pairs = [pair_index(level, level - 1)]
        x[level], msg, *more = call(
            functools.partial(up_kernel, level, pairs),
            [vec, vec] if level > 1 else [vec, vec[1:], vec[1:], (5, *vec[1:])],
            (keep, gotten, inv, inv_o, mine, other, y[level - 1], y[4], some, rest, ahead, *x[4:level:-1]),
        )
    moved = lax.ppermute(more[1], BOTH, turn_perm(n))
    lines = line_perms(n)
    order = sorted(range(1, n), key=lambda m: (m & (m + 1) != 0, m))
    got = {m: lax.ppermute(more[0], BOTH, lines[m - 1]) for m in order}
    got = [got[m] for m in range(1, n)]
    out = jax.ShapeDtypeStruct((levels, 1, count, width), jnp.bfloat16)
    return pl.pallas_call(
        functools.partial(out_kernel, n),
        out_shape=[out, out],
        in_specs=[VMEM] * (n + 5),
        out_specs=[ANY] * 2,
        scratch_shapes=[pltpu.VMEM(out.shape, out.dtype)] * 2 + [pltpu.SemaphoreType.DMA((2,))],
        compiler_params=ROOM,
    )(msg, *got, *y[:4], moved)


def solution(mesh):
    return jax.shard_map(
        on_device,
        mesh=mesh,
        in_specs=(
            P(None, "row", None, None),
            P(None, "col", "row", None, None),
            P(None, "col", "row"),
            P(None, "row", None, None),
        ),
        out_specs=(P(None, "row", None, None), P(None, "row", None, None)),
        check_vma=False,
    )
```

```python
import functools

import jax
import jax.numpy as jnp
from jax import lax
from jax.experimental import pallas as pl
from jax.experimental.pallas import tpu as pltpu
from jax.sharding import PartitionSpec as P

BOTH = ("row", "col")
NT = (((1,), (1,)), ((), ()))
NN = (((1,), (0,)), ((), ()))


def pair_index(later, earlier):
    return later * (later - 1) // 2 + earlier


def perm(n, target):
    pairs = []
    for q in range(n):
        for k in range(2):
            for z in range(n):
                a, b, c = target(q, k, z)
                assert (a, b, c) != (q, k, z)
                pairs.append(((2 * q + k) * n + z, (2 * a + b) * n + c))
    return pairs


def down_perms(n):
    return [perm(n, lambda q, k, z, j=j: (z, (q & 1) ^ 1, 2 * ((q >> 1) ^ j) + k)) for j in range(n // 2)]


def up_perms(n):
    return [perm(n, lambda q, k, z, j=j: (2 * ((z >> 1) ^ j) + k, (z & 1) ^ 1, q)) for j in reversed(range(n // 2))]


def plane_perms(n):
    return [perm(n, lambda q, k, z, m=m: (q ^ m, k ^ 1, z)) for m in range(1, n)]


def line_perms(n):
    return [perm(n, lambda q, k, z, m=m: (q, k ^ 1, z ^ m)) for m in range(1, n)]


def turn_perm(n):
    return perm(n, lambda q, k, z: (z, k ^ 1, q ^ (n - 1)))


def far_perm(n):
    return perm(n, lambda q, k, z: (z ^ (n - 1), k ^ 1, q))


def core_perm(n):
    return perm(n, lambda q, k, z: (q, k ^ 1, z))


def tree(parts):
    while len(parts) > 1:
        half = len(parts) // 2
        parts = [parts[i] + parts[i + half] for i in range(half)]
    return parts[0]


def f32(x):
    return x.astype(jnp.float32)


def bf16(x):
    return x.astype(jnp.bfloat16)


def dot(a, b, dims):
    return lax.dot_general(a, b, dims, preferred_element_type=jnp.float32)


def place():
    row = lax.axis_index("row")
    return row % 2, row // 2 == lax.axis_index("col")


def row_of(mask, p, t):
    return mask[3, pl.ds(2 * p + t, 1), :]


def lower_part(k, pairs, solved, mine, other, keep, gotten):
    outs = []
    for t in range(2):
        acc = None
        for p, y in zip(pairs, solved, strict=True):
            a = dot(y[k], mine[p, t], NT) * row_of(keep, p, t)
            b = dot(y[1 - k], other[p, t], NT) * row_of(gotten, p, t)
            acc = a + b if acc is None else acc + (a + b)
        outs.append(acc)
    return outs


def upper_part(pairs, solved, mine, other, keep, gotten):
    outs = []
    for blocks, mask in ((mine, keep), (other, gotten)):
        acc = None
        for p, x in zip(pairs, solved, strict=True):
            for t in range(2):
                a = dot(x[t], blocks[p, t], NN) * row_of(mask, p, t)
                acc = a if acc is None else acc + a
        outs.append(acc)
    return outs


def start_kernel(pattern, rhs, inv, last, mine, keep_ref, give_ref, last_ref):
    low = last.shape[1] // 2
    last_ref[:low] = last[0, low:, :]
    last_ref[low:, :low] = last[0, : low // 2, :low]
    last_ref[low:, low:] = last[0, low // 2 : low, :low]
    y = bf16(dot(rhs[0], inv[0], NT))
    keep_ref[0] = f32(y)
    for t in range(2):
        keep_ref[1 + t] = dot(y, mine[0, t], NT) * f32(pattern[t, 0, 0])
    for i in range(keep_ref.shape[1]):
        value = f32(pattern[i % 2, 0, i // 2]) if i < 2 * pattern.shape[2] else 0.0
        keep_ref[3, pl.ds(i, 1), :] = jnp.full((1, keep_ref.shape[2]), value, jnp.float32)
    give_ref[...] = keep_ref[...]


def start_all(sems, moves):
    copies = [pltpu.make_async_copy(a, b, sems.at[i]) for i, (a, b) in enumerate(moves)]
    for copy in copies:
        copy.start()
    return copies


def near_kernel(mine, keep_in, gotten_in, inv_in, other_in, keep, gotten, inv, other, y_ref, sum_ref, sems):
    pairs = [pair_index(2, 0), pair_index(2, 1)]
    moves = [(keep_in, keep), (gotten_in, gotten), (inv_in.at[1], inv.at[1])]
    copies = start_all(sems, moves + [(other_in.at[p], other.at[p]) for p in pairs])
    for copy in copies:
        copy.wait()
    k, _ = place()
    y_ref[k], y_ref[1 - k] = bf16(keep[0]), bf16(gotten[0])
    for t, part in enumerate(lower_part(k, pairs[:1], [y_ref], mine, other, keep, gotten)):
        sum_ref[t] = part


def rest_kernel(keep, gotten, mine, y0, y1, inv_in, other_in, inv, other, sum_ref, sems):
    pairs = [pair_index(3, 0), pair_index(3, 1)]
    order = pairs + [p for p in range(other.shape[0]) if p not in pairs]
    moves = [(other_in.at[p], other.at[p]) for p in order] + [(inv_in.at[i], inv.at[i]) for i in range(inv.shape[0])]
    copies = start_all(sems, moves)
    for copy in copies[:2]:
        copy.wait()
    for t, part in enumerate(lower_part(place()[0], pairs, [y0, y1], mine, other, keep, gotten)):
        sum_ref[t] = part
    for copy in copies[2:]:
        copy.wait()


def ahead_kernel(keep, gotten, mine, other, y0, y1, y2, sum_ref):
    pairs = [pair_index(4, b) for b in range(3)]
    for t, part in enumerate(lower_part(place()[0], pairs, [y0, y1, y2], mine, other, keep, gotten)):
        sum_ref[t] = part


def down_kernel(level, pair, *refs):
    keep, gotten, rhs, rhs_other, inv, inv_other, mine, other, ahead, some, rest = refs[:11]
    y_ref, msg_ref, total_ref = refs[11:]
    k, diagonal = place()
    total_ref[...] = f32(some[...]) + f32(rest[...])
    for at, b, inverse in ((k, rhs, inv), (1 - k, rhs_other, inv_other)):
        y_ref[at] = bf16(dot(bf16(f32(b[level]) - total_ref[at]), inverse[level], NT))
    parts = lower_part(k, [pair], [y_ref], mine, other, keep, gotten)
    parts = [ahead[t] + part for t, part in enumerate(parts)]
    if level == 3:
        total_ref[k], total_ref[1 - k] = f32(rhs[4]), f32(rhs_other[4])
        parts = [jnp.where(diagonal, p - total_ref[t], p) for t, p in enumerate(parts)]
    for t, part in enumerate(parts):
        msg_ref[t] = bf16(part)


def above_kernel(pairs, *refs):
    keep, gotten, mine, other = refs[:4]
    for i, part in enumerate(upper_part(pairs, refs[4:-1], mine, other, keep, gotten)):
        refs[-1][i] = part


def up_parts(k, diagonal, level, pairs, solved, y, factors, inv, inv_other, ahead=None):
    parts = upper_part(pairs, solved, *factors)
    if ahead is not None:
        parts = [ahead[i] + part for i, part in enumerate(parts)]
    outs = []
    for part, at, inverse in zip(parts, (k, 1 - k), (inv, inv_other), strict=True):
        part = jnp.where(diagonal, part - f32(y[at]), part)
        outs.append((at, bf16(dot(bf16(part), inverse[level], NN))))
    return outs


def turn_kernel(n, pairs, *refs):
    keep, gotten, inv_k, inv_o, inv, inv_other, mine, other, y3, own = refs[:10]
    got = refs[10 : 10 + n - 1]
    y_ref, x_ref, msg_ref, whole_k, whole_o = refs[10 + n - 1 :]
    k, diagonal = place()
    low = whole_k.shape[0] // 2
    for packed, inverse in ((inv_k, whole_k), (inv_o, whole_o)):
        inverse[low:, :] = packed[:low]
        inverse[: low // 2, :low] = packed[low:, :low]
        inverse[low // 2 : low, :low] = packed[low:, low:]
        inverse[:low, low:] = jnp.zeros_like(inverse[:low, low:])
    x_ref[...] = bf16(-tree([f32(own[...])] + [f32(g[...]) for g in got]))
    for at, inverse in ((k, whole_k), (1 - k, whole_o)):
        y_ref[at] = bf16(dot(x_ref[at], inverse[...], NT))
    for at, inverse in ((k, whole_k), (1 - k, whole_o)):
        x_ref[at] = bf16(dot(y_ref[at], inverse[...], NN))
    for at, part in up_parts(k, diagonal, 3, pairs, [x_ref], y3, (mine, other, keep, gotten), inv, inv_other):
        msg_ref[at] = part


def up_kernel(level, pairs, *refs):
    keep, gotten, inv, inv_other, mine, other, below, y4, some, rest, ahead = refs[:11]
    later = refs[11 : 15 - level]
    outs = refs[15 - level :]
    k, diagonal = place()
    x_ref = outs[0]
    x_ref[...] = bf16(-(f32(some[...]) + f32(rest[...])))
    solved = list(later) + [x_ref]
    factors = (mine, other, keep, gotten)
    parts = up_parts(k, diagonal, level - 1, pairs, [x_ref], below, factors, inv, inv_other, ahead)
    if level > 1:
        for at, part in parts:
            outs[1][at] = part
    else:
        for ref, (_, part) in zip(outs[1:], parts, strict=False):
            ref[...] = part
        for i, v in enumerate((y4, *solved[1:])):
            outs[3][i] = v[1 - k]


def out_kernel(n, *refs):
    own, got = refs[0], refs[1:n]
    y, moved, inv = refs[n : n + 4], refs[n + 4], refs[n + 5]
    forward, solved, forward_ref, solved_ref, sems = refs[n + 6 :]
    k, _ = place()
    for level in range(4):
        forward_ref[level, 0] = y[level][k]
    for i in range(1, 4):
        solved_ref[4 - i, 0] = moved[i]
    forward_ref[4, 0] = moved[0]
    solved_ref[4, 0] = bf16(dot(moved[0], inv[4], NN))
    solved_ref[0, 0] = bf16(-tree([f32(own[...])] + [f32(g[...]) for g in got]))
    copies = [
        pltpu.make_async_copy(forward_ref, forward, sems.at[0]),
        pltpu.make_async_copy(solved_ref, solved, sems.at[1]),
    ]
    for copy in copies:
        copy.start()
    for copy in copies:
        copy.wait()


VMEM = pl.BlockSpec(memory_space=pltpu.VMEM)
ANY = pl.BlockSpec(memory_space=pl.ANY)
ROOM = pltpu.CompilerParams(vmem_limit_bytes=16 * 1024 * 1024)


def call(body, outs, args, scratch=(), dtype=jnp.bfloat16):
    return pl.pallas_call(
        body,
        out_shape=[jax.ShapeDtypeStruct(s, dtype) for s in outs],
        in_specs=[VMEM] * len(args),
        out_specs=[VMEM] * len(outs),
        scratch_shapes=list(scratch),
        compiler_params=ROOM,
    )(*args)


def on_device(rhs, factor, pattern, diag_inverse):
    n = lax.axis_size("col")
    levels, own, count, width = rhs.shape
    assert levels == 5 and own == 1 and factor.shape[1] == 2 and lax.axis_size("row") == 2 * n

    rhs, inv = rhs[:, 0], diag_inverse[:, 0]
    mine = factor[:, :, 0]
    swap = functools.partial(lax.ppermute, axis_name=BOTH, perm=core_perm(n))
    send = lambda x, perms: [lax.ppermute(x, BOTH, p) for p in perms]
    vec, slots = (2, count, width), (4, count, width)

    def share(msg, perms):
        got = send(msg, perms)
        some = bf16(tree([f32(g) for g in got]))
        return got, some, swap(some)

    first = lambda x, at: pl.BlockSpec((1, *x.shape[1:]), lambda i: (at,) + (0,) * (len(x.shape) - 1))
    keep, give, last = pl.pallas_call(
        start_kernel,
        grid=(1,),
        out_shape=[jax.ShapeDtypeStruct(slots, jnp.float32)] * 2 + [jax.ShapeDtypeStruct((3 * width // 4, width), inv.dtype)],
        in_specs=[pl.BlockSpec(memory_space=pltpu.SMEM), first(rhs, 0), first(inv, 0), first(inv, 4), first(mine, 0)],
        out_specs=[VMEM] * 3,
        compiler_params=pltpu.CompilerParams(vmem_limit_bytes=61 * 1024 * 1024),
    )(pattern.transpose(1, 2, 0), rhs, inv, inv, mine)
    gotten = swap(give)
    msg = bf16(keep[1:3] + gotten[1:3])
    inv_s, mine_s, rhs_s, _ = lax.optimization_barrier((inv, mine, rhs, msg))
    inv_o, other, rhs_o = swap(inv_s), swap(mine_s), swap(rhs_s)
    inv_to = lax.ppermute(last, BOTH, far_perm(n))

    y = [None] * 5
    x = [None] * 5
    for level in range(1, 4):
        got, some, rest = share(msg, down_perms(n))
        early, solved, _ = lax.optimization_barrier(((inv_o, other), y[:level], got[0]))
        if level == 1:
            inv_near, other_near = early
            keep, gotten, inv_near, other_near, y[0], ahead = pl.pallas_call(
                near_kernel,
                out_shape=[jax.ShapeDtypeStruct(a.shape, a.dtype) for a in (keep, gotten, inv_o, other)]
                + [jax.ShapeDtypeStruct(vec, jnp.bfloat16), jax.ShapeDtypeStruct(vec, jnp.float32)],
                in_specs=[VMEM] + [ANY] * 4,
                out_specs=[VMEM] * 6,
                scratch_shapes=[pltpu.SemaphoreType.DMA((5,))],
                compiler_params=ROOM,
            )(mine, keep, gotten, *early)
            held = inv_near, other_near
        elif level == 2:
            *held, ahead = pl.pallas_call(
                rest_kernel,
                out_shape=[jax.ShapeDtypeStruct(a.shape, a.dtype) for a in (inv_o, other)]
                + [jax.ShapeDtypeStruct(vec, jnp.float32)],
                in_specs=[VMEM] * 5 + [ANY] * 2,
                out_specs=[VMEM] * 3,
                scratch_shapes=[pltpu.SemaphoreType.DMA((inv_o.shape[0] + other.shape[0],))],
                compiler_params=ROOM,
            )(keep, gotten, mine, *solved, *early)
            inv_o, other = held
        else:
            (ahead,) = call(ahead_kernel, [vec], (keep, gotten, mine, other, *solved), dtype=jnp.float32)
        y[level], msg = call(
            functools.partial(down_kernel, level, pair_index(level + 1, level)),
            [vec, vec],
            (keep, gotten, rhs, rhs_o, inv, held[0], mine, held[1], ahead, some, rest),
            [pltpu.VMEM(vec, jnp.float32)],
        )
        if level == 1:
            msg, inv_to = lax.optimization_barrier((msg, inv_to))
            inv_tk = swap(inv_to)
    got = send(msg, plane_perms(n))
    y[4], x[4], msg = call(
        functools.partial(turn_kernel, n, [pair_index(4, 3)]),
        [vec, vec, vec],
        (keep, gotten, inv_tk, inv_to, inv, inv_o, mine, other, y[3], msg, *got),
        [pltpu.VMEM((width, width), inv.dtype)] * 2,
    )
    for level in (3, 2, 1):
        got, some, rest = share(msg, up_perms(n))
        later, _ = lax.optimization_barrier((x[4:level:-1], got[0]))
        pairs = [pair_index(c, level - 1) for c in range(4, level, -1)]
        (ahead,) = call(
            functools.partial(above_kernel, pairs), [vec], (keep, gotten, mine, other, *later), dtype=jnp.float32
        )
        pairs = [pair_index(level, level - 1)]
        x[level], msg, *more = call(
            functools.partial(up_kernel, level, pairs),
            [vec, vec] if level > 1 else [vec, vec[1:], vec[1:], slots],
            (keep, gotten, inv, inv_o, mine, other, y[level - 1], y[4], some, rest, ahead, *x[4:level:-1]),
        )
    moved = lax.ppermute(more[1], BOTH, turn_perm(n))
    lines = line_perms(n)
    order = sorted(range(1, n), key=lambda m: (m & (m + 1) != 0, m))
    got = {m: lax.ppermute(more[0], BOTH, lines[m - 1]) for m in order}
    got = [got[m] for m in range(1, n)]
    out = jax.ShapeDtypeStruct((levels, 1, count, width), jnp.bfloat16)
    return pl.pallas_call(
        functools.partial(out_kernel, n),
        out_shape=[out, out],
        in_specs=[VMEM] * (n + 6),
        out_specs=[ANY] * 2,
        scratch_shapes=[pltpu.VMEM(out.shape, out.dtype)] * 2 + [pltpu.SemaphoreType.DMA((2,))],
        compiler_params=ROOM,
    )(msg, *got, *y[:4], moved, inv)


def solution(mesh):
    return jax.shard_map(
        on_device,
        mesh=mesh,
        in_specs=(
            P(None, "row", None, None),
            P(None, "col", "row", None, None),
            P(None, "col", "row"),
            P(None, "row", None, None),
        ),
        out_specs=(P(None, "row", None, None), P(None, "row", None, None)),
        check_vma=False,
    )
```
